32 devices in a mesh: dp: 16 (over z, x, core), tensor: 2 (over y).
Axes of the slice: x: 2, y: 2, z: 4, core: 2. Of those that a mesh axis runs over, the one named last changes fastest.
Arguments:
- tokens: bfloat16 [4096, 1024], P('dp'), may hold values from -6 to 6
- cotangent: bfloat16 [4096, 1024], P('dp'), may hold values from -6 to 6
- lengths: int32 [4], replicated, may hold values from 1 to 32, 64 in all
- norm_gains: bfloat16 [2, 1024], replicated, may hold values from 0.5 to 1.5
- query_key_weight: bfloat16 [1024, 2, 1024], P('dp', None, 'tensor'), may hold values from -0.1875 to 0.1875
- value_gate_weight: bfloat16 [1024, 2, 2048], P('dp', None, 'tensor'), may hold values from -0.1875 to 0.1875
- decay_beta_weight: bfloat16 [1024, 2, 8], P('dp', None, 'tensor'), may hold values from -0.1875 to 0.1875
- conv_query_key: bfloat16 [4, 2, 1024], P(None, None, 'tensor'), may hold values from -3 to 3
- conv_value: bfloat16 [4, 2048], P(None, 'tensor'), may hold values from -3 to 3
- decay_log: float32 [8], P('tensor'), may hold values from -6 to -1.5
- decay_bias: float32 [8], P('tensor'), may hold values from -2 to 1
- output_gain: bfloat16 [256], replicated, may hold values from 0.5 to 1.5
- out_weight: bfloat16 [1024, 2048], P('dp', 'tensor'), may hold values from -0.25 to 0.25
- gate_up_weight: bfloat16 [1024, 2, 2816], P('dp', None, 'tensor'), may hold values from -0.1875 to 0.1875
- down_weight: bfloat16 [1024, 2816], P('dp', 'tensor'), may hold values from -0.21875 to 0.21875
Outputs:
- output: bfloat16 [4096, 1024], P('dp')
- grad_tokens: float32 [4096, 1024], P('dp')
- grad_norm_gains: float32 [2, 1024], replicated
- grad_query_key: float32 [1024, 2, 1024], P('dp', None, 'tensor')
- grad_value_gate: float32 [1024, 2, 2048], P('dp', None, 'tensor')
- grad_decay_beta: float32 [1024, 2, 8], P('dp', None, 'tensor')
- grad_conv_query_key: float32 [4, 2, 1024], P(None, None, 'tensor')
- grad_conv_value: float32 [4, 2048], P(None, 'tensor')
- grad_decay_log: float32 [8], P('tensor')
- grad_decay_bias: float32 [8], P('tensor')
- grad_output_gain: float32 [256], replicated
- grad_out_weight: float32 [1024, 2048], P('dp', 'tensor')
- grad_gate_up: float32 [1024, 2, 2816], P('dp', None, 'tensor')
- grad_down: float32 [1024, 2816], P('dp', 'tensor')
The draws below stay inside these ranges and needn't reach their ends.
Inputs may be any that keep to these rules, and one draw needn't show every extreme that they name: Each sequence's length in blocks of 64 tokens; the lengths sum to 64 and the longest is exactly 32.
All inputs are finite; a program needn't handle non-finite values.
Results may differ from the reference program's by a relative error of at most 0.013.
The reference program's roundings to bfloat16 on the way count: a program that leaves them out, or rounds other values in their place, can miss the bound.
Values may be sent and summed in bfloat16 or wider, within the bound.
A program may use at most 448 MiB of HBM per device.

```python
import math
import jax
import jax.numpy as jnp
import numpy as np
from jax import lax

D = 1024
H = 8
DK = 128
DV = 256
FF = 2816
KC = 4
GROUP = 64
LONGEST = 2048
TOKENS = 4096
NSEQ = 4


def level_of(key, extent, shards, low, high):
    gain, own = 1.0, jax.random.fold_in(key, 6)
    for position, shards_of in shards:
        steps = jnp.exp(jax.random.uniform(jax.random.fold_in(own, position), (shards_of,), jnp.float32, low / len(shards), high / len(shards)))
        gain = gain * jnp.repeat(steps, extent[position] // shards_of).reshape([-1 if axis == position else 1 for axis in range(len(extent))])
    return gain


def profile(amount, total, reach, skew):
    loads = [(1 << 20) // math.isqrt(rank ** skew) + 1 for rank in range(2, amount + 1)]
    rest, given = total - reach - (amount - 1), [1] * (amount - 1)
    while rest > 0:
        movable = [i for i in range(amount - 1) if given[i] < reach]
        mass, budget = sum([loads[i] for i in movable]), rest
        for i in movable:
            addition = min(reach - given[i], max(1, budget * loads[i] // mass), rest)
            given[i] = given[i] + addition
            rest = rest - addition
    return np.array([reach] + given)


def ragged(rng, amount, total, bound, slope):
    if amount == 2:
        one = jax.random.randint(rng, (), max(1, total - bound), min(bound, total - 1) + 1)
        return jnp.stack([one, total - one])
    sizes = jnp.asarray(profile(amount, total, bound, slope), jnp.int32)
    twos = (amount - 1) // 2
    donor, taker = sizes[1:1 + 2 * twos:2], sizes[2:2 + 2 * twos:2]
    room = jnp.minimum(donor - 1, bound - taker)
    moved = jax.random.randint(jax.random.fold_in(rng, 1), (twos,), 0, 1 << 20) % (room + 1)
    sizes = sizes.at[1:1 + 2 * twos:2].set(donor - moved).at[2:2 + 2 * twos:2].set(taker + moved)
    return sizes[jax.random.permutation(jax.random.fold_in(rng, 2), amount)]


def scatter_about(own_key, shape, width, limit, split=(), kind=jnp.bfloat16):
    drawn = width * jax.random.normal(own_key, shape, jnp.float32)
    if split:
        drawn = drawn * level_of(own_key, shape, split, -0.22, 0.18)
    return jnp.clip(drawn, -limit, limit).astype(kind)


def setup_inputs(seed: int = 0) -> dict:
    keys = jax.random.split(jax.random.key(seed), 16)
    tokens = scatter_about(keys[0], (TOKENS, D), 1.0, 6.0, ((0, 16),))
    cotangent = scatter_about(keys[1], (TOKENS, D), 1.0, 6.0, ((0, 16),))
    lengths = ragged(keys[2], NSEQ, TOKENS // GROUP, LONGEST // GROUP, 1).astype(jnp.int32)
    norm_gains = jnp.clip(1.0 + 0.1 * jax.random.normal(keys[3], (2, D), jnp.float32), 0.5, 1.5).astype(jnp.bfloat16)
    query_key_weight = scatter_about(keys[4], (D, 2, H * DK), D ** -0.5, 0.1875, ((0, 16), (2, 2)))
    value_gate_weight = scatter_about(keys[5], (D, 2, H * DV), D ** -0.5, 0.1875, ((0, 16), (2, 2)))
    decay_beta_weight = scatter_about(keys[6], (D, 2, H), D ** -0.5, 0.1875, ((0, 16), (2, 2)))
    conv_query_key = scatter_about(keys[7], (KC, 2, H * DK), KC ** -0.5, 3.0, ((2, 2),))
    conv_value = scatter_about(keys[8], (KC, H * DV), KC ** -0.5, 3.0, ((1, 2),))
    decay_log = jnp.clip(-6.0 + 4.5 * jax.random.uniform(keys[9], (H,), jnp.float32) ** level_of(keys[9], (H,), ((0, 2),), -0.2, 0.2), -6.0, -1.5)
    decay_bias = jnp.clip(-2.0 + 3.0 * jax.random.uniform(keys[10], (H,), jnp.float32) ** level_of(keys[10], (H,), ((0, 2),), -0.2, 0.2), -2.0, 1.0)
    output_gain = jnp.clip(1.0 + 0.1 * jax.random.normal(keys[11], (DV,), jnp.float32), 0.5, 1.5).astype(jnp.bfloat16)
    out_weight = scatter_about(keys[12], (D, H * DV), (H * DV // 4) ** -0.5, 0.25, ((0, 16), (1, 2)))
    gate_up_weight = scatter_about(keys[13], (D, 2, FF), D ** -0.5, 0.1875, ((0, 16), (2, 2)))
    down_weight = scatter_about(keys[14], (D, FF), (FF // 4) ** -0.5, 0.21875, ((0, 16), (1, 2)))
    return dict(tokens=tokens, cotangent=cotangent, lengths=lengths, norm_gains=norm_gains, query_key_weight=query_key_weight, value_gate_weight=value_gate_weight, decay_beta_weight=decay_beta_weight, conv_query_key=conv_query_key, conv_value=conv_value, decay_log=decay_log, decay_bias=decay_bias, output_gain=output_gain, out_weight=out_weight, gate_up_weight=gate_up_weight, down_weight=down_weight)


high_accuracy_mode = lax.Precision.HIGHEST

@jax.custom_vjp
def low(v):
    return lax.optimization_barrier(v.astype(jnp.bfloat16)).astype(jnp.float32)

@jax.custom_vjp
def low_back(v):
    return v

def low_keep(v):
    return (low(v), None)

def low_pass(kept, grad):
    return (grad,)

def back_keep(v):
    return (v, None)

def back_low(kept, grad):
    return (low(grad),)
low.defvjp(low_keep, low_pass)
low_back.defvjp(back_keep, back_low)

def unit_rows(values, epsilon):
    return values * lax.rsqrt(lax.optimization_barrier(jnp.mean(values * values, axis=-1, keepdims=True)) + epsilon)

def unit_sphere(values):
    return values * lax.rsqrt(lax.optimization_barrier(jnp.sum(values * values, axis=-1, keepdims=True)) + 1e-06)

def to_blocks(rows_data, size):
    count = rows_data.shape[0] // size
    return rows_data.reshape(count, size, rows_data.shape[1], -1).transpose(0, 2, 1, 3)

def from_blocks(blocked):
    return blocked.transpose(0, 2, 1, 3).reshape(-1, blocked.shape[1], blocked.shape[3])

def group_parts(key_rows, value_rows, beta_rows, log_decay):
    length = key_rows.shape[1]
    running_decay_total = jnp.cumsum(log_decay, axis=-1)
    row_index = lax.broadcasted_iota(jnp.int32, (length, length), 0)
    col_index = lax.broadcasted_iota(jnp.int32, (length, length), 1)
    spread = running_decay_total[:, :, None] - running_decay_total[:, None, :]
    ratio = jnp.where(row_index >= col_index, jnp.exp(jnp.minimum(spread, 0.0)), 0.0)
    strict = jnp.where(row_index > col_index, ratio, 0.0)
    inner = jnp.einsum('hck,hdk->hcd', key_rows, key_rows, precision=high_accuracy_mode)
    system = jnp.eye(length, dtype=jnp.float32) + beta_rows[:, :, None] * strict * inner
    decay = jnp.exp(running_decay_total)
    right = jnp.concatenate([beta_rows[:, :, None] * value_rows, (beta_rows * decay)[:, :, None] * key_rows], axis=-1)
    solved = lax.linalg.triangular_solve(system, right, left_side=True, lower=True)
    vwidth = value_rows.shape[-1]
    return (running_decay_total, ratio, decay, solved[..., :vwidth], solved[..., vwidth:])

def group_out(state_sequence, query_rows_local, key_rows, value_rows, beta_rows, log_decay, keep_flag):
    state_sequence = state_sequence * keep_flag
    running_decay_total, ratio, decay, solved_value_rows, solved_weight_rows = group_parts(key_rows, value_rows, beta_rows, log_decay)
    newly_written_state = solved_value_rows - jnp.einsum('pel,pln->pen', solved_weight_rows, state_sequence, precision=high_accuracy_mode)
    scores = jnp.einsum('hck,hdk->hcd', query_rows_local, key_rows, precision=high_accuracy_mode) * ratio
    carried_over_state = jnp.einsum('pel,pln->pen', query_rows_local, state_sequence, precision=high_accuracy_mode)
    result = (decay[:, :, None] * carried_over_state + jnp.einsum('hcd,hdv->hcv', scores, newly_written_state, precision=high_accuracy_mode)) * query_rows_local.shape[-1] ** (-0.5)
    trailing_rows = jnp.exp(running_decay_total[:, -1:] - running_decay_total)[:, :, None] * key_rows
    refreshed_state = jnp.exp(running_decay_total[:, -1])[:, None, None] * state_sequence + jnp.einsum('ypt,ypr->ytr', trailing_rows, newly_written_state, precision=high_accuracy_mode)
    return (refreshed_state, result)

def advance(state_sequence, pieces):
    return group_out(state_sequence, *pieces)

def forward(tokens, norm_gains, query_key_weight, value_gate_weight, decay_beta_weight, conv_query_key, conv_value, decay_log, decay_bias, output_gain, out_weight, gate_up_weight, down_weight, seg_first, keep_flags):
    total = tokens.shape[0]
    normed = low(unit_rows(tokens, 1e-06) * norm_gains[0])
    proj_qk = low(low_back(jnp.dot(normed, query_key_weight.reshape(D, 2 * H * DK), precision=high_accuracy_mode)))
    proj_vg = low_back(jnp.dot(normed, value_gate_weight.reshape(D, 2 * H * DV), precision=high_accuracy_mode))
    proj_ab = low_back(jnp.dot(normed, decay_beta_weight.reshape(D, 2 * H), precision=high_accuracy_mode))
    pre_conv = jnp.concatenate([proj_qk, low(proj_vg[:, :H * DV])], axis=1)
    gate_raw = proj_vg[:, H * DV:]
    conv_taps = jnp.concatenate([conv_query_key.reshape(KC, 2 * H * DK), conv_value], axis=1)
    positions = jnp.arange(total, dtype=jnp.int32)
    conv_sum = jnp.zeros_like(pre_conv)
    for tap_index in range(KC):
        offset = KC - 1 - tap_index
        shifted = jnp.concatenate([jnp.zeros((offset, pre_conv.shape[1]), pre_conv.dtype), pre_conv[:total - offset]], axis=0)
        inside = (positions - offset >= seg_first).astype(pre_conv.dtype)[:, None]
        conv_sum = conv_sum + conv_taps[tap_index] * shifted * inside
    activated = jax.nn.silu(conv_sum)
    query_rows_local = low(unit_sphere(activated[:, :H * DK].reshape(total, H, DK)))
    key_rows = low(unit_sphere(activated[:, H * DK:2 * H * DK].reshape(total, H, DK)))
    value_rows = low(activated[:, 2 * H * DK:].reshape(total, H, DV))
    beta_rows = jax.nn.sigmoid(proj_ab[:, H:])
    log_decay = -jnp.exp(decay_log) * jax.nn.softplus(proj_ab[:, :H] + decay_bias)
    pieces = (to_blocks(query_rows_local, GROUP), to_blocks(key_rows, GROUP), to_blocks(value_rows, GROUP), to_blocks(beta_rows[:, :, None], GROUP)[..., 0], to_blocks(log_decay[:, :, None], GROUP)[..., 0], keep_flags)
    initial = jnp.zeros((H, DK, DV), jnp.float32)
    unused, blocked = lax.scan(jax.checkpoint(advance), initial, pieces)
    heads_out = from_blocks(blocked)
    gated = unit_rows(heads_out, 1e-05) * output_gain * jax.nn.silu(gate_raw.reshape(total, H, DV))
    gated_low = low(gated.reshape(total, H * DV))
    mixed = low_back(jnp.dot(gated_low, out_weight.T, precision=high_accuracy_mode))
    residual = tokens + mixed
    normed_two = low(unit_rows(residual, 1e-06) * norm_gains[1])
    up_gate = low_back(jnp.dot(normed_two, gate_up_weight.reshape(D, 2 * FF), precision=high_accuracy_mode))
    hidden = low(jax.nn.silu(up_gate[:, :FF]) * up_gate[:, FF:])
    return residual + jnp.dot(hidden, down_weight.T, precision=high_accuracy_mode)

def reference(tokens, cotangent, lengths, norm_gains, query_key_weight, value_gate_weight, decay_beta_weight, conv_query_key, conv_value, decay_log, decay_bias, output_gain, out_weight, gate_up_weight, down_weight):
    total = tokens.shape[0]
    starts = ((jnp.cumsum(lengths) - lengths) * GROUP).astype(jnp.int32)
    positions = jnp.arange(total, dtype=jnp.int32)
    seg_first = lax.optimization_barrier(jnp.max(jnp.where(starts[None, :] <= positions[:, None], starts[None, :], 0), axis=1)).astype(jnp.int32)
    block_first = positions[::GROUP]
    keep_flags = 1.0 - jnp.any(starts[None, :] == block_first[:, None], axis=1).astype(jnp.float32)
    floats = tuple((item.astype(jnp.float32) for item in (tokens, norm_gains, query_key_weight, value_gate_weight, decay_beta_weight, conv_query_key, conv_value, decay_log, decay_bias, output_gain, out_weight, gate_up_weight, down_weight)))

    def whole(*params):
        return forward(*params, seg_first, keep_flags)
    result, backward = jax.vjp(whole, *floats)
    grads = backward(cotangent.astype(jnp.float32))
    return (result.astype(jnp.bfloat16), grads[0], grads[1], grads[2], grads[3], grads[4], grads[5], grads[6], grads[7], grads[8], grads[9], grads[10], grads[11], grads[12])
```

```python
import jax
import jax.numpy as jnp
from jax import lax
from jax.sharding import PartitionSpec as P

DK = 128
DV = 256
GROUP = 64


LONGEST_BLOCKS = 32

accuracy = lax.Precision.HIGH


def shifted(block, axis, distance):
    devices = range(lax.axis_size(axis))
    route = [(i - distance, i) for i in devices if i - distance in devices]
    return lax.ppermute(block, axis, route)


def round_low(values):
    return lax.optimization_barrier(values.astype(jnp.bfloat16)).astype(jnp.float32)


def unit_rows(values, epsilon):
    return values * lax.rsqrt(jnp.mean(values * values, axis=-1, keepdims=True) + epsilon)


def unit_sphere(values):
    return values * lax.rsqrt(jnp.sum(values * values, axis=-1, keepdims=True) + 1e-06)


def norm_back(grad_unit, unit_value, scale_rows):
    return scale_rows * (
        grad_unit - unit_value * jnp.mean(grad_unit * unit_value, axis=-1, keepdims=True)
    )


def to_blocks(rows_data, size):
    count = rows_data.shape[0] // size
    return rows_data.reshape(count, size, rows_data.shape[1], -1).transpose(0, 2, 1, 3)


def from_blocks(blocked):
    return blocked.transpose(0, 2, 1, 3).reshape(-1, blocked.shape[1], blocked.shape[3])


def matmul(left, right):
    return jnp.einsum("...ij,...jk->...ik", left, right, precision=accuracy)


def matmul_tn(left, right):
    return jnp.einsum("...ji,...jk->...ik", left, right, precision=accuracy)


def matmul_nt(left, right):
    return jnp.einsum("...ij,...kj->...ik", left, right, precision=accuracy)


def pair_sum(part, axis):
    if lax.axis_size(axis) != 2:
        return lax.psum(part, axis).astype(jnp.float32)
    other = lax.ppermute(part, axis, [(0, 1), (1, 0)])
    return part.astype(jnp.float32) + other.astype(jnp.float32)


def carried(mat, vec, axis, direction, window):
    size = mat.shape[-1]
    packed = jnp.concatenate([mat, vec], axis=-1).astype(jnp.bfloat16)
    window = min(window, lax.axis_size(axis) - 1)
    total = shifted(packed, axis, direction).astype(jnp.float32)
    reach = 1
    while reach < window:
        low = total.astype(jnp.bfloat16)
        last = 2 * reach >= window
        if last:
            low = low[..., size:]
        far = shifted(low, axis, direction * reach).astype(jnp.float32)
        product = matmul(total[..., :size], far)
        if last:
            return product + total[..., size:]
        total = product + jnp.concatenate(
            [jnp.zeros_like(total[..., :size]), total[..., size:]], axis=-1
        )
        reach = 2 * reach
    return total[..., size:]


def inverse_of(system):
    length = system.shape[-1]
    row = lax.broadcasted_iota(jnp.int32, (length, length), 0)
    col = lax.broadcasted_iota(jnp.int32, (length, length), 1)
    inverse = None
    half = 1
    while half < length:
        mask = (row // (2 * half) == col // (2 * half)) & (row // half > col // half)
        corner = jnp.where(mask, system, 0.0)
        if inverse is None:
            inverse = jnp.eye(length, dtype=jnp.float32) - corner
        else:
            inverse = inverse - matmul(matmul(inverse, corner), inverse)
        half = 2 * half
    return inverse


@jax.custom_vjp
def solve(system, right):
    return matmul(inverse_of(system), right)


def solve_keep(system, right):
    inverse = inverse_of(system)
    solved = matmul(inverse, right)
    return solved, (inverse, solved)


def solve_back(kept, grad):
    inverse, solved = kept
    grad_right = matmul_tn(inverse, grad)
    return -matmul_nt(grad_right, solved), grad_right


solve.defvjp(solve_keep, solve_back)


def block_parts(queries, keys, values, betas, log_decay):
    length = keys.shape[-2]
    key_size = keys.shape[-1]
    row = lax.broadcasted_iota(jnp.int32, (length, length), 0)
    col = lax.broadcasted_iota(jnp.int32, (length, length), 1)
    running = jnp.einsum(
        "...c,cd->...d",
        log_decay,
        (row <= col).astype(jnp.float32),
        precision=lax.Precision.HIGHEST,
    )
    spread = running[..., :, None] - running[..., None, :]
    ratio = jnp.where(row >= col, jnp.exp(jnp.minimum(spread, 0.0)), 0.0)
    strict = jnp.where(row > col, ratio, 0.0)
    products = matmul_nt(jnp.concatenate([keys, queries], axis=-2), keys)
    inner, across = products[..., :length, :], products[..., length:, :]
    system = jnp.eye(length, dtype=jnp.float32) + betas[..., None] * strict * inner
    decay = jnp.exp(running)
    right = jnp.concatenate(
        [(betas * decay)[..., None] * keys, betas[..., None] * values], axis=-1
    )
    solved = solve(system, right)
    trailing = jnp.exp(running[..., -1:] - running)[..., None] * keys
    written = matmul_tn(trailing, solved)
    step_a = (
        jnp.exp(running[..., -1])[..., None, None] * jnp.eye(key_size, dtype=jnp.float32)
        - written[..., :key_size]
    )
    scale = key_size ** (-0.5)
    return (
        step_a,
        written[..., key_size:],
        solved[..., :key_size],
        solved[..., key_size:],
        scale * across * ratio,
        scale * decay[..., None] * queries,
    )


def front(extended, proj_ab, conv_taps, decay_log, decay_bias, inside):
    row_count = proj_ab.shape[0]
    head_count = decay_log.shape[0]
    taps = conv_taps.shape[0]
    conv_sum = conv_taps[0] * extended[0:row_count] * inside[0]
    for tap_index in range(1, taps):
        conv_sum = (
            conv_sum
            + conv_taps[tap_index] * extended[tap_index : tap_index + row_count] * inside[tap_index]
        )
    activated = jax.nn.silu(conv_sum)
    width_k = head_count * DK
    query_rows_local = unit_sphere(activated[:, :width_k].reshape(row_count, head_count, DK))
    key_rows = unit_sphere(activated[:, width_k : 2 * width_k].reshape(row_count, head_count, DK))
    value_rows = activated[:, 2 * width_k :].reshape(row_count, head_count, DV)
    beta_rows = jax.nn.sigmoid(proj_ab[:, head_count:])
    log_decay = -jnp.exp(decay_log) * jax.nn.softplus(proj_ab[:, :head_count] + decay_bias)
    return (query_rows_local, key_rows, value_rows, beta_rows, log_decay)


def gated_output(heads_out, gate_raw, output_gain):
    gate_heads = gate_raw.reshape(heads_out.shape)
    return (unit_rows(heads_out, 1e-05) * output_gain * jax.nn.silu(gate_heads)).reshape(
        gate_raw.shape
    )


def contract_rows(left, right):
    return lax.dot_general(
        left, right, (((0,), (0,)), ((), ())), preferred_element_type=jnp.float32
    )


def contract_cols(left, right):
    return lax.dot_general(
        left, right, (((1,), (1,)), ((), ())), preferred_element_type=jnp.float32
    )


def summed_rows(left, right):
    part = contract_rows(left, right).astype(jnp.bfloat16)
    share = lax.psum_scatter(part, "dp", scatter_dimension=0, tiled=True)
    return share.astype(jnp.float32)


def local(
    tokens,
    cotangent,
    lengths,
    norm_gains,
    query_key_weight,
    value_gate_weight,
    decay_beta_weight,
    conv_query_key,
    conv_value,
    decay_log,
    decay_bias,
    output_gain,
    out_weight,
    gate_up_weight,
    down_weight,
):
    row_count, width = tokens.shape
    head_count = decay_log.shape[0]
    width_k = head_count * DK
    width_v = head_count * DV
    taps = conv_query_key.shape[0]
    rim_rows = taps - 1
    first_row = lax.axis_index("dp") * row_count
    positions = first_row + lax.broadcasted_iota(jnp.int32, (row_count,), 0)
    seq_starts = (jnp.cumsum(lengths) - lengths) * GROUP
    seg_first = jnp.max(
        jnp.where(seq_starts[None, :] <= positions[:, None], seq_starts[None, :], 0), axis=1
    )
    block_first = positions[::GROUP]
    keep_flags = 1.0 - jnp.any(seq_starts[None, :] == block_first[:, None], axis=1).astype(
        jnp.float32
    )
    inside = jnp.stack(
        [
            (positions - (rim_rows - tap_index) >= seg_first).astype(jnp.float32)[:, None]
            for tap_index in range(taps)
        ]
    )
    gains = norm_gains.astype(jnp.float32)
    inputs = tokens.astype(jnp.float32)
    scale_one = lax.rsqrt(jnp.mean(inputs * inputs, axis=-1, keepdims=True) + 1e-06)
    unit_one = inputs * scale_one
    normed = (unit_one * gains[0]).astype(jnp.bfloat16)
    full_in = lax.all_gather(
        jnp.concatenate(
            [
                query_key_weight.reshape(-1, 2 * width_k),
                value_gate_weight.reshape(-1, 2 * width_v),
                decay_beta_weight.reshape(-1, 2 * head_count),
            ],
            axis=1,
        ),
        "dp",
        axis=0,
        tiled=True,
    )
    full_out = lax.all_gather(out_weight, "dp", axis=0, tiled=True)
    width_c = 2 * width_k + width_v
    width_g = width_c + width_v
    projected = jnp.dot(normed, full_in, preferred_element_type=jnp.float32)
    pre_conv = projected[:, :width_c].astype(jnp.bfloat16)
    gate_raw = projected[:, width_c:width_g]
    proj_ab = projected[:, width_g:]
    rim = shifted(pre_conv[row_count - rim_rows :], "dp", 1)
    extended = jnp.concatenate([rim, pre_conv], axis=0).astype(jnp.float32)
    conv_taps = jnp.concatenate(
        [conv_query_key.reshape(taps, 2 * width_k), conv_value], axis=1
    ).astype(jnp.float32)

    def front_piece(ext_rows, ab_rows, tap_rows, log_rate, rate_bias):
        return front(ext_rows, ab_rows, tap_rows, log_rate, rate_bias, inside)

    fronted, front_back = jax.vjp(front_piece, extended, proj_ab, conv_taps, decay_log, decay_bias)
    query_rows_local, key_rows, value_rows, beta_rows, log_decay = fronted
    block_q = to_blocks(round_low(query_rows_local), GROUP)
    block_k = to_blocks(round_low(key_rows), GROUP)
    block_v = to_blocks(round_low(value_rows), GROUP)
    block_b = to_blocks(beta_rows[:, :, None], GROUP)[..., 0]
    block_g = to_blocks(log_decay[:, :, None], GROUP)[..., 0]

    parts, parts_back = jax.vjp(block_parts, block_q, block_k, block_v, block_b, block_g)
    step_a, step_b, erase, write, scores, reads = parts
    keep = keep_flags[:, None, None, None]
    block_count = step_a.shape[0]
    window = -(-(LONGEST_BLOCKS - 1) // block_count)
    kept_a = keep * step_a
    maps = [jnp.concatenate([kept_a[0], step_b[0]], axis=-1)]
    no_map = jnp.zeros_like(kept_a[0])
    for j in range(1, block_count):
        maps.append(
            matmul(kept_a[j], maps[-1]) + jnp.concatenate([no_map, step_b[j]], axis=-1)
        )
    entering = carried(maps[-1][..., :DK], maps[-1][..., DK:], "dp", 1, window)
    states = entering[None]
    if block_count > 1:
        before = jnp.stack(maps[:-1])
        states = jnp.concatenate(
            [states, matmul(before[..., :DK], entering[None]) + before[..., DK:]], axis=0
        )
    seen = keep * states
    recalled = matmul(jnp.concatenate([erase, reads], axis=-2), seen)
    fresh = write - recalled[..., :GROUP, :]
    block_out = recalled[..., GROUP:, :] + matmul(scores, fresh)
    heads_out = from_blocks(block_out)
    gated, gated_back = jax.vjp(gated_output, heads_out, gate_raw, output_gain.astype(jnp.float32))
    gated_low = gated.astype(jnp.bfloat16)
    mixed_sum = pair_sum(contract_cols(gated_low, full_out).astype(jnp.bfloat16), "tensor")
    residual = inputs + mixed_sum
    scale_two = lax.rsqrt(jnp.mean(residual * residual, axis=-1, keepdims=True) + 1e-06)
    unit_two = residual * scale_two
    normed_two = (unit_two * gains[1]).astype(jnp.bfloat16)
    ff_local = down_weight.shape[1]
    matrix_gu = lax.all_gather(
        gate_up_weight.reshape(-1, 2 * ff_local), "dp", axis=0, tiled=True
    )
    full_down = lax.all_gather(down_weight, "dp", axis=0, tiled=True)
    up_gate = jnp.dot(normed_two, matrix_gu, preferred_element_type=jnp.float32)
    gate_two = up_gate[:, :ff_local]
    up_two = up_gate[:, ff_local:]
    hidden = (jax.nn.silu(gate_two) * up_two).astype(jnp.bfloat16)
    mlp_total = pair_sum(contract_cols(hidden, full_down).astype(jnp.bfloat16), "tensor")
    output = (residual + mlp_total).astype(jnp.bfloat16)
    grad_out = cotangent.astype(jnp.float32)
    grad_hidden = jnp.dot(cotangent, full_down, preferred_element_type=jnp.float32)
    share_down = summed_rows(cotangent, hidden)
    sigma_two = jax.nn.sigmoid(gate_two)
    grad_gate_two = grad_hidden * up_two * sigma_two * (1.0 + gate_two * (1.0 - sigma_two))
    grad_up_two = grad_hidden * gate_two * sigma_two
    grad_gu_low = jnp.concatenate([grad_gate_two, grad_up_two], axis=1).astype(jnp.bfloat16)
    share_gu = summed_rows(normed_two, grad_gu_low)
    grad_normed_two_part = contract_cols(grad_gu_low, matrix_gu)
    grad_normed_two = pair_sum(grad_normed_two_part.astype(jnp.bfloat16), "tensor")
    gain_two_grad = jnp.sum(grad_normed_two * unit_two, axis=0)
    grad_residual = grad_out + norm_back(grad_normed_two * gains[1], unit_two, scale_two)
    grad_res_low = grad_residual.astype(jnp.bfloat16)
    grad_gated = jnp.dot(grad_res_low, full_out, preferred_element_type=jnp.float32)
    share_out = summed_rows(grad_res_low, gated_low)
    grad_heads, grad_gate_raw, grad_gain_part = gated_back(grad_gated)
    grad_blocks = to_blocks(grad_heads, GROUP)
    grad_fresh = matmul_tn(scores, grad_blocks)
    both = jnp.concatenate([-grad_fresh, grad_blocks], axis=-2)
    grad_seen = keep * matmul_tn(jnp.concatenate([erase, reads], axis=-2), both)
    flipped = jnp.swapaxes(kept_a, -1, -2)
    maps_back = [jnp.concatenate([flipped[-1], grad_seen[-1]], axis=-1)]
    for j in range(block_count - 2, -1, -1):
        maps_back.append(
            matmul(flipped[j], maps_back[-1]) + jnp.concatenate([no_map, grad_seen[j]], axis=-1)
        )
    leaving = carried(maps_back[-1][..., :DK], maps_back[-1][..., DK:], "dp", -1, window)
    grad_states = leaving[None]
    if block_count > 1:
        after = jnp.stack(maps_back[-2::-1])
        grad_states = jnp.concatenate(
            [matmul(after[..., :DK], leaving[None]) + after[..., DK:], grad_states], axis=0
        )
    grad_factors = matmul_nt(both, seen)
    grad_bq, grad_bk, grad_bv, grad_bb, grad_bg = parts_back(
        (
            matmul_nt(grad_states, seen),
            grad_states,
            grad_factors[..., :GROUP, :],
            grad_fresh,
            matmul_nt(grad_blocks, fresh),
            grad_factors[..., GROUP:, :],
        )
    )
    grad_queries = from_blocks(grad_bq)
    grad_keys = from_blocks(grad_bk)
    grad_values = from_blocks(grad_bv)
    grad_betas = from_blocks(grad_bb[..., None])[..., 0]
    grad_decays = from_blocks(grad_bg[..., None])[..., 0]
    grad_ext, grad_ab, grad_taps, grad_decay_log, grad_decay_bias = front_back(
        (grad_queries, grad_keys, grad_values, grad_betas, grad_decays)
    )
    rim_grad = shifted(grad_ext[:rim_rows], "dp", -1)
    grad_pre = grad_ext[rim_rows:] + jnp.concatenate(
        [jnp.zeros((row_count - rim_rows, grad_ext.shape[1]), jnp.float32), rim_grad], axis=0
    )
    grad_pre_low = grad_pre.astype(jnp.bfloat16)
    grad_in_low = jnp.concatenate(
        [grad_pre_low, grad_gate_raw.astype(jnp.bfloat16), grad_ab.astype(jnp.bfloat16)], axis=1
    )
    share_in = summed_rows(normed, grad_in_low)
    grad_normed = pair_sum(contract_cols(grad_in_low, full_in).astype(jnp.bfloat16), "tensor")
    grad_gain_out = pair_sum(grad_gain_part, "tensor")
    gain_one_grad = jnp.sum(grad_normed * unit_one, axis=0)
    grad_tokens = grad_residual + norm_back(grad_normed * gains[0], unit_one, scale_one)
    small_parts = (
        gain_one_grad,
        gain_two_grad,
        grad_taps[:, : 2 * width_k].reshape(-1),
        grad_taps[:, 2 * width_k :].reshape(-1),
        grad_gain_out,
        grad_decay_log,
        grad_decay_bias,
    )
    small = lax.psum(jnp.concatenate(small_parts), "dp")
    sums = []
    at = 0
    for part in small_parts:
        sums.append(small[at : at + part.shape[0]])
        at += part.shape[0]
    return (
        output,
        grad_tokens,
        jnp.stack(sums[:2]),
        share_in[:, : 2 * width_k].reshape(query_key_weight.shape),
        share_in[:, 2 * width_k : width_g].reshape(value_gate_weight.shape),
        share_in[:, width_g:].reshape(decay_beta_weight.shape),
        sums[2].reshape(conv_query_key.shape),
        sums[3].reshape(conv_value.shape),
        sums[5],
        sums[6],
        sums[4],
        share_out,
        share_gu.reshape(gate_up_weight.shape),
        share_down,
    )


def solution(mesh):
    in_specs = (
        P("dp", None),
        P("dp", None),
        P(),
        P(),
        P("dp", None, "tensor"),
        P("dp", None, "tensor"),
        P("dp", None, "tensor"),
        P(None, None, "tensor"),
        P(None, "tensor"),
        P("tensor"),
        P("tensor"),
        P(),
        P("dp", "tensor"),
        P("dp", None, "tensor"),
        P("dp", "tensor"),
    )
    out_specs = (
        P("dp", None),
        P("dp", None),
        P(),
        P("dp", None, "tensor"),
        P("dp", None, "tensor"),
        P("dp", None, "tensor"),
        P(None, None, "tensor"),
        P(None, "tensor"),
        P("tensor"),
        P("tensor"),
        P(),
        P("dp", "tensor"),
        P("dp", None, "tensor"),
        P("dp", "tensor"),
    )
    return jax.shard_map(local, mesh=mesh, in_specs=in_specs, out_specs=out_specs, check_vma=False)
```

```python
import jax
import jax.numpy as jnp
from jax import lax
from jax.sharding import PartitionSpec as P

DK = 128
DV = 256
GROUP = 64


LONGEST_BLOCKS = 32

accuracy = lax.Precision.HIGH


def shifted(block, axis, distance):
    devices = range(lax.axis_size(axis))
    route = [(i - distance, i) for i in devices if i - distance in devices]
    return lax.ppermute(block, axis, route)


def round_low(values):
    return lax.optimization_barrier(values.astype(jnp.bfloat16)).astype(jnp.float32)


def unit_rows(values, epsilon):
    return values * lax.rsqrt(jnp.mean(values * values, axis=-1, keepdims=True) + epsilon)


def unit_sphere(values):
    return values * lax.rsqrt(jnp.sum(values * values, axis=-1, keepdims=True) + 1e-06)


def norm_back(grad_unit, unit_value, scale_rows):
    return scale_rows * (
        grad_unit - unit_value * jnp.mean(grad_unit * unit_value, axis=-1, keepdims=True)
    )


def to_blocks(rows_data, size):
    count = rows_data.shape[0] // size
    return rows_data.reshape(count, size, rows_data.shape[1], -1).transpose(0, 2, 1, 3)


def from_blocks(blocked):
    return blocked.transpose(0, 2, 1, 3).reshape(-1, blocked.shape[1], blocked.shape[3])


def matmul(left, right):
    return jnp.einsum("...ij,...jk->...ik", left, right, precision=accuracy)


def matmul_tn(left, right):
    return jnp.einsum("...ji,...jk->...ik", left, right, precision=accuracy)


def matmul_nt(left, right):
    return jnp.einsum("...ij,...kj->...ik", left, right, precision=accuracy)


def pair_sum(part, axis):
    if lax.axis_size(axis) != 2:
        return lax.psum(part, axis).astype(jnp.float32)
    other = lax.ppermute(part, axis, [(0, 1), (1, 0)])
    return part.astype(jnp.float32) + other.astype(jnp.float32)


def carried(mat, vec, axis, direction, window):
    size = mat.shape[-1]
    packed = jnp.concatenate([mat, vec], axis=-1).astype(jnp.bfloat16)
    window = min(window, lax.axis_size(axis) - 1)
    total = shifted(packed, axis, direction).astype(jnp.float32)
    reach = 1
    while reach < window:
        low = total.astype(jnp.bfloat16)
        last = 2 * reach >= window
        if last:
            low = low[..., size:]
        far = shifted(low, axis, direction * reach).astype(jnp.float32)
        product = matmul(total[..., :size], far)
        if last:
            return product + total[..., size:]
        total = product + jnp.concatenate(
            [jnp.zeros_like(total[..., :size]), total[..., size:]], axis=-1
        )
        reach = 2 * reach
    return total[..., size:]


def inverse_of(system):
    length = system.shape[-1]
    row = lax.broadcasted_iota(jnp.int32, (length, length), 0)
    col = lax.broadcasted_iota(jnp.int32, (length, length), 1)
    inverse = None
    half = 1
    while half < length:
        mask = (row // (2 * half) == col // (2 * half)) & (row // half > col // half)
        corner = jnp.where(mask, system, 0.0)
        if inverse is None:
            inverse = jnp.eye(length, dtype=jnp.float32) - corner
        else:
            inverse = inverse - matmul(matmul(inverse, corner), inverse)
        half = 2 * half
    return inverse


@jax.custom_vjp
def solve(system, right):
    return matmul(inverse_of(system), right)


def solve_keep(system, right):
    inverse = inverse_of(system)
    solved = matmul(inverse, right)
    return solved, (inverse, solved)


def solve_back(kept, grad):
    inverse, solved = kept
    grad_right = matmul_tn(inverse, grad)
    return -matmul_nt(grad_right, solved), grad_right


solve.defvjp(solve_keep, solve_back)


def block_parts(queries, keys, values, betas, log_decay):
    length = keys.shape[-2]
    key_size = keys.shape[-1]
    row = lax.broadcasted_iota(jnp.int32, (length, length), 0)
    col = lax.broadcasted_iota(jnp.int32, (length, length), 1)
    running = jnp.einsum(
        "...c,cd->...d",
        log_decay,
        (row <= col).astype(jnp.float32),
        precision=lax.Precision.HIGHEST,
    )
    spread = running[..., :, None] - running[..., None, :]
    ratio = jnp.where(row >= col, jnp.exp(jnp.minimum(spread, 0.0)), 0.0)
    strict = jnp.where(row > col, ratio, 0.0)
    products = matmul_nt(jnp.concatenate([keys, queries], axis=-2), keys)
    inner, across = products[..., :length, :], products[..., length:, :]
    system = jnp.eye(length, dtype=jnp.float32) + betas[..., None] * strict * inner
    decay = jnp.exp(running)
    right = jnp.concatenate(
        [(betas * decay)[..., None] * keys, betas[..., None] * values], axis=-1
    )
    solved = solve(system, right)
    trailing = jnp.exp(running[..., -1:] - running)[..., None] * keys
    written = matmul_tn(trailing, solved)
    step_a = (
        jnp.exp(running[..., -1])[..., None, None] * jnp.eye(key_size, dtype=jnp.float32)
        - written[..., :key_size]
    )
    scale = key_size ** (-0.5)
    return (
        step_a,
        written[..., key_size:],
        solved[..., :key_size],
        solved[..., key_size:],
        scale * across * ratio,
        scale * decay[..., None] * queries,
    )


def front(extended, proj_ab, conv_taps, decay_log, decay_bias, inside):
    row_count = proj_ab.shape[0]
    head_count = decay_log.shape[0]
    taps = conv_taps.shape[0]
    conv_sum = conv_taps[0] * extended[0:row_count] * inside[0]
    for tap_index in range(1, taps):
        conv_sum = (
            conv_sum
            + conv_taps[tap_index] * extended[tap_index : tap_index + row_count] * inside[tap_index]
        )
    activated = jax.nn.silu(conv_sum)
    width_k = head_count * DK
    query_rows_local = unit_sphere(activated[:, :width_k].reshape(row_count, head_count, DK))
    key_rows = unit_sphere(activated[:, width_k : 2 * width_k].reshape(row_count, head_count, DK))
    value_rows = activated[:, 2 * width_k :].reshape(row_count, head_count, DV)
    beta_rows = jax.nn.sigmoid(proj_ab[:, head_count:])
    log_decay = -jnp.exp(decay_log) * jax.nn.softplus(proj_ab[:, :head_count] + decay_bias)
    return (query_rows_local, key_rows, value_rows, beta_rows, log_decay)


def gated_output(heads_out, gate_raw, output_gain):
    gate_heads = gate_raw.reshape(heads_out.shape)
    return (unit_rows(heads_out, 1e-05) * output_gain * jax.nn.silu(gate_heads)).reshape(
        gate_raw.shape
    )


def contract_rows(left, right):
    return lax.dot_general(
        left, right, (((0,), (0,)), ((), ())), preferred_element_type=jnp.float32
    )


def contract_cols(left, right):
    return lax.dot_general(
        left, right, (((1,), (1,)), ((), ())), preferred_element_type=jnp.float32
    )


def ring_place(axis):
    chips = lax.axis_size(axis) // 2
    cycle = list(range(0, chips, 2)) + list(range(1, chips, 2))[::-1]
    orders = [cycle, cycle[::-1]]
    route = []
    for core in range(2):
        for i in range(chips):
            source, target = orders[core][i], orders[core][(i + 1) % chips]
            route.append((2 * source + core, 2 * target + core))
    mine = lax.axis_index(axis)
    core = mine % 2
    places = [[order.index(chip) for chip in range(chips)] for order in orders]
    place = jnp.asarray(places, jnp.int32)[core, mine // 2]

    def chip_behind(back):
        return jnp.asarray(orders, jnp.int32)[core, (place - back) % chips]

    return route, core, chip_behind


def uses_ring(axis):
    size = lax.axis_size(axis)
    return size % 4 == 0 and 4 <= size <= 16


def gathered_rows(part, axis):
    if not uses_ring(axis):
        return lax.all_gather(part, axis, axis=0, tiled=True)
    size = lax.axis_size(axis)
    route, core, chip_behind = ring_place(axis)
    held = jnp.zeros((size // 2,) + part.shape, part.dtype)
    moving = part
    for step in range(size // 2):
        if step:
            moving = lax.ppermute(moving, axis, route)
        held = lax.dynamic_update_index_in_dim(held, moving, chip_behind(step), 0)
    other = lax.ppermute(held, axis, [(i, i ^ 1) for i in range(size)])
    first = core == 0
    both = jnp.stack([jnp.where(first, held, other), jnp.where(first, other, held)], axis=1)
    return both.reshape(size * part.shape[0], part.shape[1])


def scattered_rows(part, axis):
    if not uses_ring(axis):
        return lax.psum_scatter(part, axis, scatter_dimension=0, tiled=True)
    size = lax.axis_size(axis)
    route, core, chip_behind = ring_place(axis)
    cut = part.reshape(size // 2, 2, part.shape[0] // size, part.shape[1])
    other = lax.ppermute(
        lax.dynamic_index_in_dim(cut, 1 - core, 1, keepdims=False),
        axis,
        [(i, i ^ 1) for i in range(size)],
    )
    own = lax.dynamic_index_in_dim(cut, core, 1, keepdims=False)
    pair = (own.astype(jnp.float32) + other.astype(jnp.float32)).astype(part.dtype)
    moving = lax.dynamic_index_in_dim(pair, chip_behind(1), 0, keepdims=False)
    for step in range(1, size // 2):
        moving = lax.ppermute(moving, axis, route).astype(jnp.float32)
        mine = lax.dynamic_index_in_dim(pair, chip_behind(1 + step), 0, keepdims=False)
        moving = moving + mine.astype(jnp.float32)
        if step < size // 2 - 1:
            moving = moving.astype(part.dtype)
    return moving


def doubled_sum(values, axis):
    size = lax.axis_size(axis)
    if size & (size - 1):
        return lax.psum(values, axis)
    distance = 1
    while distance < size:
        values = values + lax.ppermute(values, axis, [(i, i ^ distance) for i in range(size)])
        distance = 2 * distance
    return values


def summed_rows(left, right):
    part = contract_rows(left, right).astype(jnp.bfloat16)
    share = lax.psum_scatter(part, "dp", scatter_dimension=0, tiled=True)
    return share.astype(jnp.float32)


def local(
    tokens,
    cotangent,
    lengths,
    norm_gains,
    query_key_weight,
    value_gate_weight,
    decay_beta_weight,
    conv_query_key,
    conv_value,
    decay_log,
    decay_bias,
    output_gain,
    out_weight,
    gate_up_weight,
    down_weight,
):
    row_count, width = tokens.shape
    head_count = decay_log.shape[0]
    width_k = head_count * DK
    width_v = head_count * DV
    taps = conv_query_key.shape[0]
    rim_rows = taps - 1
    first_row = lax.axis_index("dp") * row_count
    positions = first_row + lax.broadcasted_iota(jnp.int32, (row_count,), 0)
    seq_starts = (jnp.cumsum(lengths) - lengths) * GROUP
    seg_first = jnp.max(
        jnp.where(seq_starts[None, :] <= positions[:, None], seq_starts[None, :], 0), axis=1
    )
    block_first = positions[::GROUP]
    keep_flags = 1.0 - jnp.any(seq_starts[None, :] == block_first[:, None], axis=1).astype(
        jnp.float32
    )
    inside = jnp.stack(
        [
            (positions - (rim_rows - tap_index) >= seg_first).astype(jnp.float32)[:, None]
            for tap_index in range(taps)
        ]
    )
    gains = norm_gains.astype(jnp.float32)
    inputs = tokens.astype(jnp.float32)
    scale_one = lax.rsqrt(jnp.mean(inputs * inputs, axis=-1, keepdims=True) + 1e-06)
    unit_one = inputs * scale_one
    normed = (unit_one * gains[0]).astype(jnp.bfloat16)
    full_in = gathered_rows(
        jnp.concatenate(
            [
                query_key_weight.reshape(-1, 2 * width_k),
                value_gate_weight.reshape(-1, 2 * width_v),
                decay_beta_weight.reshape(-1, 2 * head_count),
            ],
            axis=1,
        ),
        "dp",
    )
    full_out = lax.all_gather(out_weight, "dp", axis=0, tiled=True)
    width_c = 2 * width_k + width_v
    width_g = width_c + width_v
    projected = jnp.dot(normed, full_in, preferred_element_type=jnp.float32)
    pre_conv = projected[:, :width_c].astype(jnp.bfloat16)
    gate_raw = projected[:, width_c:width_g]
    proj_ab = projected[:, width_g:]
    rim = shifted(pre_conv[row_count - rim_rows :], "dp", 1)
    extended = jnp.concatenate([rim, pre_conv], axis=0).astype(jnp.float32)
    conv_taps = jnp.concatenate(
        [conv_query_key.reshape(taps, 2 * width_k), conv_value], axis=1
    ).astype(jnp.float32)

    def front_piece(ext_rows, ab_rows, tap_rows, log_rate, rate_bias):
        return front(ext_rows, ab_rows, tap_rows, log_rate, rate_bias, inside)

    fronted, front_back = jax.vjp(front_piece, extended, proj_ab, conv_taps, decay_log, decay_bias)
    query_rows_local, key_rows, value_rows, beta_rows, log_decay = fronted
    block_q = to_blocks(round_low(query_rows_local), GROUP)
    block_k = to_blocks(round_low(key_rows), GROUP)
    block_v = to_blocks(round_low(value_rows), GROUP)
    block_b = to_blocks(beta_rows[:, :, None], GROUP)[..., 0]
    block_g = to_blocks(log_decay[:, :, None], GROUP)[..., 0]

    parts, parts_back = jax.vjp(block_parts, block_q, block_k, block_v, block_b, block_g)
    step_a, step_b, erase, write, scores, reads = parts
    keep = keep_flags[:, None, None, None]
    block_count = step_a.shape[0]
    window = -(-(LONGEST_BLOCKS - 1) // block_count)
    kept_a = keep * step_a
    maps = [jnp.concatenate([kept_a[0], step_b[0]], axis=-1)]
    no_map = jnp.zeros_like(kept_a[0])
    for j in range(1, block_count):
        maps.append(
            matmul(kept_a[j], maps[-1]) + jnp.concatenate([no_map, step_b[j]], axis=-1)
        )
    entering = carried(maps[-1][..., :DK], maps[-1][..., DK:], "dp", 1, window)
    states = entering[None]
    if block_count > 1:
        before = jnp.stack(maps[:-1])
        states = jnp.concatenate(
            [states, matmul(before[..., :DK], entering[None]) + before[..., DK:]], axis=0
        )
    seen = keep * states
    recalled = matmul(jnp.concatenate([erase, reads], axis=-2), seen)
    fresh = write - recalled[..., :GROUP, :]
    block_out = recalled[..., GROUP:, :] + matmul(scores, fresh)
    heads_out = from_blocks(block_out)
    gated, gated_back = jax.vjp(gated_output, heads_out, gate_raw, output_gain.astype(jnp.float32))
    gated_low = gated.astype(jnp.bfloat16)
    mixed_sum = pair_sum(contract_cols(gated_low, full_out).astype(jnp.bfloat16), "tensor")
    residual = inputs + mixed_sum
    scale_two = lax.rsqrt(jnp.mean(residual * residual, axis=-1, keepdims=True) + 1e-06)
    unit_two = residual * scale_two
    normed_two = (unit_two * gains[1]).astype(jnp.bfloat16)
    ff_local = down_weight.shape[1]
    matrix_gu = lax.all_gather(
        gate_up_weight.reshape(-1, 2 * ff_local), "dp", axis=0, tiled=True
    )
    full_down = lax.all_gather(down_weight, "dp", axis=0, tiled=True)
    up_gate = jnp.dot(normed_two, matrix_gu, preferred_element_type=jnp.float32)
    gate_two = up_gate[:, :ff_local]
    up_two = up_gate[:, ff_local:]
    hidden = (jax.nn.silu(gate_two) * up_two).astype(jnp.bfloat16)
    mlp_total = pair_sum(contract_cols(hidden, full_down).astype(jnp.bfloat16), "tensor")
    output = (residual + mlp_total).astype(jnp.bfloat16)
    grad_out = cotangent.astype(jnp.float32)
    grad_hidden = jnp.dot(cotangent, full_down, preferred_element_type=jnp.float32)
    share_down = summed_rows(cotangent, hidden)
    sigma_two = jax.nn.sigmoid(gate_two)
    grad_gate_two = grad_hidden * up_two * sigma_two * (1.0 + gate_two * (1.0 - sigma_two))
    grad_up_two = grad_hidden * gate_two * sigma_two
    grad_gu_low = jnp.concatenate([grad_gate_two, grad_up_two], axis=1).astype(jnp.bfloat16)
    share_gu = summed_rows(normed_two, grad_gu_low)
    grad_normed_two_part = contract_cols(grad_gu_low, matrix_gu)
    grad_normed_two = pair_sum(grad_normed_two_part.astype(jnp.bfloat16), "tensor")
    gain_two_grad = jnp.sum(grad_normed_two * unit_two, axis=0)
    grad_residual = grad_out + norm_back(grad_normed_two * gains[1], unit_two, scale_two)
    grad_res_low = grad_residual.astype(jnp.bfloat16)
    grad_gated = jnp.dot(grad_res_low, full_out, preferred_element_type=jnp.float32)
    share_out = summed_rows(grad_res_low, gated_low)
    grad_heads, grad_gate_raw, grad_gain_part = gated_back(grad_gated)
    grad_blocks = to_blocks(grad_heads, GROUP)
    grad_fresh = matmul_tn(scores, grad_blocks)
    both = jnp.concatenate([-grad_fresh, grad_blocks], axis=-2)
    grad_seen = keep * matmul_tn(jnp.concatenate([erase, reads], axis=-2), both)
    flipped = jnp.swapaxes(kept_a, -1, -2)
    maps_back = [jnp.concatenate([flipped[-1], grad_seen[-1]], axis=-1)]
    for j in range(block_count - 2, -1, -1):
        maps_back.append(
            matmul(flipped[j], maps_back[-1]) + jnp.concatenate([no_map, grad_seen[j]], axis=-1)
        )
    leaving = carried(maps_back[-1][..., :DK], maps_back[-1][..., DK:], "dp", -1, window)
    grad_states = leaving[None]
    if block_count > 1:
        after = jnp.stack(maps_back[-2::-1])
        grad_states = jnp.concatenate(
            [matmul(after[..., :DK], leaving[None]) + after[..., DK:], grad_states], axis=0
        )
    grad_factors = matmul_nt(both, seen)
    grad_bq, grad_bk, grad_bv, grad_bb, grad_bg = parts_back(
        (
            matmul_nt(grad_states, seen),
            grad_states,
            grad_factors[..., :GROUP, :],
            grad_fresh,
            matmul_nt(grad_blocks, fresh),
            grad_factors[..., GROUP:, :],
        )
    )
    grad_queries = from_blocks(grad_bq)
    grad_keys = from_blocks(grad_bk)
    grad_values = from_blocks(grad_bv)
    grad_betas = from_blocks(grad_bb[..., None])[..., 0]
    grad_decays = from_blocks(grad_bg[..., None])[..., 0]
    grad_ext, grad_ab, grad_taps, grad_decay_log, grad_decay_bias = front_back(
        (grad_queries, grad_keys, grad_values, grad_betas, grad_decays)
    )
    rim_grad = shifted(grad_ext[:rim_rows], "dp", -1)
    grad_pre = grad_ext[rim_rows:] + jnp.concatenate(
        [jnp.zeros((row_count - rim_rows, grad_ext.shape[1]), jnp.float32), rim_grad], axis=0
    )
    grad_pre_low = grad_pre.astype(jnp.bfloat16)
    grad_in_low = jnp.concatenate(
        [grad_pre_low, grad_gate_raw.astype(jnp.bfloat16), grad_ab.astype(jnp.bfloat16)], axis=1
    )
    share_in = scattered_rows(
        contract_rows(normed, grad_in_low).astype(jnp.bfloat16), "dp"
    ).astype(jnp.float32)
    grad_normed = pair_sum(contract_cols(grad_in_low, full_in).astype(jnp.bfloat16), "tensor")
    grad_gain_out = pair_sum(grad_gain_part, "tensor")
    gain_one_grad = jnp.sum(grad_normed * unit_one, axis=0)
    grad_tokens = grad_residual + norm_back(grad_normed * gains[0], unit_one, scale_one)
    small_parts = (
        gain_one_grad,
        gain_two_grad,
        grad_taps[:, : 2 * width_k].reshape(-1),
        grad_taps[:, 2 * width_k :].reshape(-1),
        grad_gain_out,
        grad_decay_log,
        grad_decay_bias,
    )
    small = doubled_sum(jnp.concatenate(small_parts), "dp")
    sums = []
    at = 0
    for part in small_parts:
        sums.append(small[at : at + part.shape[0]])
        at += part.shape[0]
    return (
        output,
        grad_tokens,
        jnp.stack(sums[:2]),
        share_in[:, : 2 * width_k].reshape(query_key_weight.shape),
        share_in[:, 2 * width_k : width_g].reshape(value_gate_weight.shape),
        share_in[:, width_g:].reshape(decay_beta_weight.shape),
        sums[2].reshape(conv_query_key.shape),
        sums[3].reshape(conv_value.shape),
        sums[5],
        sums[6],
        sums[4],
        share_out,
        share_gu.reshape(gate_up_weight.shape),
        share_down,
    )


def solution(mesh):
    in_specs = (
        P("dp", None),
        P("dp", None),
        P(),
        P(),
        P("dp", None, "tensor"),
        P("dp", None, "tensor"),
        P("dp", None, "tensor"),
        P(None, None, "tensor"),
        P(None, "tensor"),
        P("tensor"),
        P("tensor"),
        P(),
        P("dp", "tensor"),
        P("dp", None, "tensor"),
        P("dp", "tensor"),
    )
    out_specs = (
        P("dp", None),
        P("dp", None),
        P(),
        P("dp", None, "tensor"),
        P("dp", None, "tensor"),
        P("dp", None, "tensor"),
        P(None, None, "tensor"),
        P(None, "tensor"),
        P("tensor"),
        P("tensor"),
        P(),
        P("dp", "tensor"),
        P("dp", None, "tensor"),
        P("dp", "tensor"),
    )
    return jax.shard_map(local, mesh=mesh, in_specs=in_specs, out_specs=out_specs, check_vma=False)
```

```python
import jax
import jax.numpy as jnp
from jax import lax
from jax.sharding import PartitionSpec as P

DK = 128
DV = 256
GROUP = 64


LONGEST_BLOCKS = 32

accuracy = lax.Precision.HIGH


def shifted(block, axis, distance):
    devices = range(lax.axis_size(axis))
    route = [(i - distance, i) for i in devices if i - distance in devices]
    return lax.ppermute(block, axis, route)


def round_low(values):
    return lax.optimization_barrier(values.astype(jnp.bfloat16)).astype(jnp.float32)


def unit_rows(values, epsilon):
    return values * lax.rsqrt(jnp.mean(values * values, axis=-1, keepdims=True) + epsilon)


def unit_sphere(values):
    return values * lax.rsqrt(jnp.sum(values * values, axis=-1, keepdims=True) + 1e-06)


def norm_back(grad_unit, unit_value, scale_rows):
    return scale_rows * (
        grad_unit - unit_value * jnp.mean(grad_unit * unit_value, axis=-1, keepdims=True)
    )


def to_blocks(rows_data, size):
    count = rows_data.shape[0] // size
    return rows_data.reshape(count, size, rows_data.shape[1], -1).transpose(0, 2, 1, 3)


def from_blocks(blocked):
    return blocked.transpose(0, 2, 1, 3).reshape(-1, blocked.shape[1], blocked.shape[3])


def matmul(left, right):
    return jnp.einsum("...ij,...jk->...ik", left, right, precision=accuracy)


def matmul_tn(left, right):
    return jnp.einsum("...ji,...jk->...ik", left, right, precision=accuracy)


def matmul_nt(left, right):
    return jnp.einsum("...ij,...kj->...ik", left, right, precision=accuracy)


def pair_sum(part, axis):
    if lax.axis_size(axis) != 2:
        return lax.psum(part, axis).astype(jnp.float32)
    other = lax.ppermute(part, axis, [(0, 1), (1, 0)])
    return part.astype(jnp.float32) + other.astype(jnp.float32)


def carried(mat, vec, axis, direction, window):
    size = mat.shape[-1]
    packed = jnp.concatenate([mat, vec], axis=-1).astype(jnp.bfloat16)
    window = min(window, lax.axis_size(axis) - 1)
    total = shifted(packed, axis, direction).astype(jnp.float32)
    reach = 1
    while reach < window:
        low = total.astype(jnp.bfloat16)
        last = 2 * reach >= window
        if last:
            low = low[..., size:]
        far = shifted(low, axis, direction * reach).astype(jnp.float32)
        product = matmul(total[..., :size], far)
        if last:
            return product + total[..., size:]
        total = product + jnp.concatenate(
            [jnp.zeros_like(total[..., :size]), total[..., size:]], axis=-1
        )
        reach = 2 * reach
    return total[..., size:]


def inverse_of(system):
    length = system.shape[-1]
    row = lax.broadcasted_iota(jnp.int32, (length, length), 0)
    col = lax.broadcasted_iota(jnp.int32, (length, length), 1)
    inverse = None
    half = 1
    while half < length:
        mask = (row // (2 * half) == col // (2 * half)) & (row // half > col // half)
        corner = jnp.where(mask, system, 0.0)
        if inverse is None:
            inverse = jnp.eye(length, dtype=jnp.float32) - corner
        else:
            inverse = inverse - matmul(matmul(inverse, corner), inverse)
        half = 2 * half
    return inverse


@jax.custom_vjp
def solve(system, right):
    return matmul(inverse_of(system), right)


def solve_keep(system, right):
    inverse = inverse_of(system)
    solved = matmul(inverse, right)
    return solved, (inverse, solved)


def solve_back(kept, grad):
    inverse, solved = kept
    grad_right = matmul_tn(inverse, grad)
    return -matmul_nt(grad_right, solved), grad_right


solve.defvjp(solve_keep, solve_back)


def block_parts(queries, keys, values, betas, log_decay):
    length = keys.shape[-2]
    key_size = keys.shape[-1]
    row = lax.broadcasted_iota(jnp.int32, (length, length), 0)
    col = lax.broadcasted_iota(jnp.int32, (length, length), 1)
    running = jnp.einsum(
        "...c,cd->...d",
        log_decay,
        (row <= col).astype(jnp.float32),
        precision=lax.Precision.HIGHEST,
    )
    spread = running[..., :, None] - running[..., None, :]
    ratio = jnp.where(row >= col, jnp.exp(jnp.minimum(spread, 0.0)), 0.0)
    strict = jnp.where(row > col, ratio, 0.0)
    products = matmul_nt(jnp.concatenate([keys, queries], axis=-2), keys)
    inner, across = products[..., :length, :], products[..., length:, :]
    system = jnp.eye(length, dtype=jnp.float32) + betas[..., None] * strict * inner
    decay = jnp.exp(running)
    right = jnp.concatenate(
        [(betas * decay)[..., None] * keys, betas[..., None] * values], axis=-1
    )
    solved = solve(system, right)
    trailing = jnp.exp(running[..., -1:] - running)[..., None] * keys
    written = matmul_tn(trailing, solved)
    step_a = (
        jnp.exp(running[..., -1])[..., None, None] * jnp.eye(key_size, dtype=jnp.float32)
        - written[..., :key_size]
    )
    scale = key_size ** (-0.5)
    return (
        step_a,
        written[..., key_size:],
        solved[..., :key_size],
        solved[..., key_size:],
        scale * across * ratio,
        scale * decay[..., None] * queries,
    )


def front(extended, proj_ab, conv_taps, decay_log, decay_bias, inside):
    row_count = proj_ab.shape[0]
    head_count = decay_log.shape[0]
    taps = conv_taps.shape[0]
    conv_sum = conv_taps[0] * extended[0:row_count] * inside[0]
    for tap_index in range(1, taps):
        conv_sum = (
            conv_sum
            + conv_taps[tap_index] * extended[tap_index : tap_index + row_count] * inside[tap_index]
        )
    activated = jax.nn.silu(conv_sum)
    width_k = head_count * DK
    query_rows_local = unit_sphere(activated[:, :width_k].reshape(row_count, head_count, DK))
    key_rows = unit_sphere(activated[:, width_k : 2 * width_k].reshape(row_count, head_count, DK))
    value_rows = activated[:, 2 * width_k :].reshape(row_count, head_count, DV)
    beta_rows = jax.nn.sigmoid(proj_ab[:, head_count:])
    log_decay = -jnp.exp(decay_log) * jax.nn.softplus(proj_ab[:, :head_count] + decay_bias)
    return (query_rows_local, key_rows, value_rows, beta_rows, log_decay)


def gated_output(heads_out, gate_raw, output_gain):
    gate_heads = gate_raw.reshape(heads_out.shape)
    return (unit_rows(heads_out, 1e-05) * output_gain * jax.nn.silu(gate_heads)).reshape(
        gate_raw.shape
    )


def contract_rows(left, right):
    return lax.dot_general(
        left, right, (((0,), (0,)), ((), ())), preferred_element_type=jnp.float32
    )


def contract_cols(left, right):
    return lax.dot_general(
        left, right, (((1,), (1,)), ((), ())), preferred_element_type=jnp.float32
    )


def doubled_sum(values, axis):
    size = lax.axis_size(axis)
    if size & (size - 1):
        return lax.psum(values, axis)
    distance = 1
    while distance < size:
        values = values + lax.ppermute(values, axis, [(i, i ^ distance) for i in range(size)])
        distance = 2 * distance
    return values


def summed_rows(left, right):
    return summed_part(contract_rows(left, right).astype(jnp.bfloat16))


def summed_part(part):
    share = lax.psum_scatter(part, "dp", scatter_dimension=0, tiled=True)
    return share.astype(jnp.float32)


def local(
    tokens,
    cotangent,
    lengths,
    norm_gains,
    query_key_weight,
    value_gate_weight,
    decay_beta_weight,
    conv_query_key,
    conv_value,
    decay_log,
    decay_bias,
    output_gain,
    out_weight,
    gate_up_weight,
    down_weight,
):
    row_count, width = tokens.shape
    head_count = decay_log.shape[0]
    width_k = head_count * DK
    width_v = head_count * DV
    taps = conv_query_key.shape[0]
    rim_rows = taps - 1
    first_row = lax.axis_index("dp") * row_count
    positions = first_row + lax.broadcasted_iota(jnp.int32, (row_count,), 0)
    seq_starts = (jnp.cumsum(lengths) - lengths) * GROUP
    seg_first = jnp.max(
        jnp.where(seq_starts[None, :] <= positions[:, None], seq_starts[None, :], 0), axis=1
    )
    block_first = positions[::GROUP]
    keep_flags = 1.0 - jnp.any(seq_starts[None, :] == block_first[:, None], axis=1).astype(
        jnp.float32
    )
    inside = jnp.stack(
        [
            (positions - (rim_rows - tap_index) >= seg_first).astype(jnp.float32)[:, None]
            for tap_index in range(taps)
        ]
    )
    gains = norm_gains.astype(jnp.float32)
    inputs = tokens.astype(jnp.float32)
    scale_one = lax.rsqrt(jnp.mean(inputs * inputs, axis=-1, keepdims=True) + 1e-06)
    unit_one = inputs * scale_one
    normed = (unit_one * gains[0]).astype(jnp.bfloat16)
    full_in = lax.all_gather(
        jnp.concatenate(
            [
                query_key_weight.reshape(-1, 2 * width_k),
                value_gate_weight.reshape(-1, 2 * width_v),
                decay_beta_weight.reshape(-1, 2 * head_count),
            ],
            axis=1,
        ),
        "dp",
        axis=0,
        tiled=True,
    )
    full_out = lax.all_gather(out_weight, "dp", axis=0, tiled=True)
    width_c = 2 * width_k + width_v
    width_g = width_c + width_v
    projected = jnp.dot(normed, full_in, preferred_element_type=jnp.float32)
    pre_conv = projected[:, :width_c].astype(jnp.bfloat16)
    gate_raw = projected[:, width_c:width_g]
    proj_ab = projected[:, width_g:]
    rim = shifted(pre_conv[row_count - rim_rows :], "dp", 1)
    extended = jnp.concatenate([rim, pre_conv], axis=0).astype(jnp.float32)
    conv_taps = jnp.concatenate(
        [conv_query_key.reshape(taps, 2 * width_k), conv_value], axis=1
    ).astype(jnp.float32)

    def front_piece(ext_rows, ab_rows, tap_rows, log_rate, rate_bias):
        return front(ext_rows, ab_rows, tap_rows, log_rate, rate_bias, inside)

    fronted, front_back = jax.vjp(front_piece, extended, proj_ab, conv_taps, decay_log, decay_bias)
    query_rows_local, key_rows, value_rows, beta_rows, log_decay = fronted
    block_q = to_blocks(round_low(query_rows_local), GROUP)
    block_k = to_blocks(round_low(key_rows), GROUP)
    block_v = to_blocks(round_low(value_rows), GROUP)
    block_b = to_blocks(beta_rows[:, :, None], GROUP)[..., 0]
    block_g = to_blocks(log_decay[:, :, None], GROUP)[..., 0]

    parts, parts_back = jax.vjp(block_parts, block_q, block_k, block_v, block_b, block_g)
    step_a, step_b, erase, write, scores, reads = parts
    keep = keep_flags[:, None, None, None]
    block_count = step_a.shape[0]
    window = -(-(LONGEST_BLOCKS - 1) // block_count)
    kept_a = keep * step_a
    maps = [jnp.concatenate([kept_a[0], step_b[0]], axis=-1)]
    no_map = jnp.zeros_like(kept_a[0])
    for j in range(1, block_count):
        maps.append(
            matmul(kept_a[j], maps[-1]) + jnp.concatenate([no_map, step_b[j]], axis=-1)
        )
    entering = carried(maps[-1][..., :DK], maps[-1][..., DK:], "dp", 1, window)
    states = entering[None]
    if block_count > 1:
        before = jnp.stack(maps[:-1])
        states = jnp.concatenate(
            [states, matmul(before[..., :DK], entering[None]) + before[..., DK:]], axis=0
        )
    seen = keep * states
    recalled = matmul(jnp.concatenate([erase, reads], axis=-2), seen)
    fresh = write - recalled[..., :GROUP, :]
    block_out = recalled[..., GROUP:, :] + matmul(scores, fresh)
    heads_out = from_blocks(block_out)
    gated, gated_back = jax.vjp(gated_output, heads_out, gate_raw, output_gain.astype(jnp.float32))
    gated_low = gated.astype(jnp.bfloat16)
    mixed_sum = pair_sum(contract_cols(gated_low, full_out).astype(jnp.bfloat16), "tensor")
    residual = inputs + mixed_sum
    scale_two = lax.rsqrt(jnp.mean(residual * residual, axis=-1, keepdims=True) + 1e-06)
    unit_two = residual * scale_two
    normed_two = (unit_two * gains[1]).astype(jnp.bfloat16)
    ff_local = down_weight.shape[1]
    matrix_gu = lax.all_gather(
        gate_up_weight.reshape(-1, 2 * ff_local), "dp", axis=0, tiled=True
    )
    full_down = lax.all_gather(down_weight, "dp", axis=0, tiled=True)
    up_gate = jnp.dot(normed_two, matrix_gu, preferred_element_type=jnp.float32)
    gate_two = up_gate[:, :ff_local]
    up_two = up_gate[:, ff_local:]
    hidden = (jax.nn.silu(gate_two) * up_two).astype(jnp.bfloat16)
    mlp_total = pair_sum(contract_cols(hidden, full_down).astype(jnp.bfloat16), "tensor")
    output = (residual + mlp_total).astype(jnp.bfloat16)
    grad_out = cotangent.astype(jnp.float32)
    grad_hidden = jnp.dot(cotangent, full_down, preferred_element_type=jnp.float32)
    part_down = contract_rows(cotangent, hidden).astype(jnp.bfloat16)
    sigma_two = jax.nn.sigmoid(gate_two)
    grad_gate_two = grad_hidden * up_two * sigma_two * (1.0 + gate_two * (1.0 - sigma_two))
    grad_up_two = grad_hidden * gate_two * sigma_two
    grad_gu_low = jnp.concatenate([grad_gate_two, grad_up_two], axis=1).astype(jnp.bfloat16)
    part_gu = contract_rows(normed_two, grad_gu_low).astype(jnp.bfloat16)
    grad_normed_two_part = contract_cols(grad_gu_low, matrix_gu)
    grad_normed_two = pair_sum(grad_normed_two_part.astype(jnp.bfloat16), "tensor")
    grad_normed_two, part_down, part_gu = lax.optimization_barrier(
        (grad_normed_two, part_down, part_gu)
    )
    share_down = summed_part(part_down)
    share_gu = summed_part(part_gu)
    gain_two_grad = jnp.sum(grad_normed_two * unit_two, axis=0)
    grad_residual = grad_out + norm_back(grad_normed_two * gains[1], unit_two, scale_two)
    grad_res_low = grad_residual.astype(jnp.bfloat16)
    grad_gated = jnp.dot(grad_res_low, full_out, preferred_element_type=jnp.float32)
    share_out = summed_rows(grad_res_low, gated_low)
    grad_heads, grad_gate_raw, grad_gain_part = gated_back(grad_gated)
    grad_blocks = to_blocks(grad_heads, GROUP)
    grad_fresh = matmul_tn(scores, grad_blocks)
    both = jnp.concatenate([-grad_fresh, grad_blocks], axis=-2)
    grad_seen = keep * matmul_tn(jnp.concatenate([erase, reads], axis=-2), both)
    flipped = jnp.swapaxes(kept_a, -1, -2)
    maps_back = [jnp.concatenate([flipped[-1], grad_seen[-1]], axis=-1)]
    for j in range(block_count - 2, -1, -1):
        maps_back.append(
            matmul(flipped[j], maps_back[-1]) + jnp.concatenate([no_map, grad_seen[j]], axis=-1)
        )
    leaving = carried(maps_back[-1][..., :DK], maps_back[-1][..., DK:], "dp", -1, window)
    grad_states = leaving[None]
    if block_count > 1:
        after = jnp.stack(maps_back[-2::-1])
        grad_states = jnp.concatenate(
            [matmul(after[..., :DK], leaving[None]) + after[..., DK:], grad_states], axis=0
        )
    grad_factors = matmul_nt(both, seen)
    grad_bq, grad_bk, grad_bv, grad_bb, grad_bg = parts_back(
        (
            matmul_nt(grad_states, seen),
            grad_states,
            grad_factors[..., :GROUP, :],
            grad_fresh,
            matmul_nt(grad_blocks, fresh),
            grad_factors[..., GROUP:, :],
        )
    )
    grad_queries = from_blocks(grad_bq)
    grad_keys = from_blocks(grad_bk)
    grad_values = from_blocks(grad_bv)
    grad_betas = from_blocks(grad_bb[..., None])[..., 0]
    grad_decays = from_blocks(grad_bg[..., None])[..., 0]
    grad_ext, grad_ab, grad_taps, grad_decay_log, grad_decay_bias = front_back(
        (grad_queries, grad_keys, grad_values, grad_betas, grad_decays)
    )
    rim_grad = shifted(grad_ext[:rim_rows], "dp", -1)
    grad_pre = grad_ext[rim_rows:] + jnp.concatenate(
        [jnp.zeros((row_count - rim_rows, grad_ext.shape[1]), jnp.float32), rim_grad], axis=0
    )
    grad_pre_low = grad_pre.astype(jnp.bfloat16)
    grad_in_low = jnp.concatenate(
        [grad_pre_low, grad_gate_raw.astype(jnp.bfloat16), grad_ab.astype(jnp.bfloat16)], axis=1
    )
    share_in = summed_rows(normed, grad_in_low)
    grad_normed = pair_sum(contract_cols(grad_in_low, full_in).astype(jnp.bfloat16), "tensor")
    grad_gain_out = pair_sum(grad_gain_part, "tensor")
    gain_one_grad = jnp.sum(grad_normed * unit_one, axis=0)
    grad_tokens = grad_residual + norm_back(grad_normed * gains[0], unit_one, scale_one)
    small_parts = (
        gain_one_grad,
        gain_two_grad,
        grad_taps[:, : 2 * width_k].reshape(-1),
        grad_taps[:, 2 * width_k :].reshape(-1),
        grad_gain_out,
        grad_decay_log,
        grad_decay_bias,
    )
    small = doubled_sum(jnp.concatenate(small_parts), "dp")
    sums = []
    at = 0
    for part in small_parts:
        sums.append(small[at : at + part.shape[0]])
        at += part.shape[0]
    return (
        output,
        grad_tokens,
        jnp.stack(sums[:2]),
        share_in[:, : 2 * width_k].reshape(query_key_weight.shape),
        share_in[:, 2 * width_k : width_g].reshape(value_gate_weight.shape),
        share_in[:, width_g:].reshape(decay_beta_weight.shape),
        sums[2].reshape(conv_query_key.shape),
        sums[3].reshape(conv_value.shape),
        sums[5],
        sums[6],
        sums[4],
        share_out,
        share_gu.reshape(gate_up_weight.shape),
        share_down,
    )


def solution(mesh):
    in_specs = (
        P("dp", None),
        P("dp", None),
        P(),
        P(),
        P("dp", None, "tensor"),
        P("dp", None, "tensor"),
        P("dp", None, "tensor"),
        P(None, None, "tensor"),
        P(None, "tensor"),
        P("tensor"),
        P("tensor"),
        P(),
        P("dp", "tensor"),
        P("dp", None, "tensor"),
        P("dp", "tensor"),
    )
    out_specs = (
        P("dp", None),
        P("dp", None),
        P(),
        P("dp", None, "tensor"),
        P("dp", None, "tensor"),
        P("dp", None, "tensor"),
        P(None, None, "tensor"),
        P(None, "tensor"),
        P("tensor"),
        P("tensor"),
        P(),
        P("dp", "tensor"),
        P("dp", None, "tensor"),
        P("dp", "tensor"),
    )
    return jax.shard_map(local, mesh=mesh, in_specs=in_specs, out_specs=out_specs, check_vma=False)
```
